32 devices in a mesh: dp: 16 (over z, x, core), fsdp: 2 (over y).
Axes of the slice: x: 2, y: 2, z: 4, core: 2. Of those that a mesh axis runs over, the one named last changes fastest.
Arguments:
- tokens: bfloat16 [12288, 8192], P(('dp', 'fsdp')), may hold values from -41 to 41
- norm_gain: bfloat16 [8192], replicated, may hold values from 0.099609375 to 1.8984375
- key_weight: bfloat16 [8192, 768], P('fsdp'), may hold values from -0.0625 to 0.0625
- key_cotangent: bfloat16 [12288, 768], P(('dp', 'fsdp')), may hold values from -0.125 to 0.125
- basis: bfloat16 [768, 512], replicated, may hold values from -0.21875 to 0.21875
- exp_avg: float32 [512, 8192], P('dp', 'fsdp'), may hold values from -4 to 4
- exp_avg_sq: float32 [512, 8192], P('dp', 'fsdp'), may hold values from 0.2 to 2
Outputs:
- keys: bfloat16 [12288, 768], P(('dp', 'fsdp'))
- new_exp_avg: float32 [512, 8192], P('dp', 'fsdp')
- new_exp_avg_sq: float32 [512, 8192], P('dp', 'fsdp')
- update: bfloat16 [8192, 768], P('fsdp')
The draws below stay inside these ranges and needn't reach their ends.
All inputs are finite; a program needn't handle non-finite values.
Results may differ from the reference program's by a relative error of at most 0.0051.
Values may be sent and summed in bfloat16 or wider, within the bound.
A program may use at most 128 MiB of HBM per device.

```python
import math
import jax
import jax.numpy as jnp
from jax import lax

D = 8192
KV = 768
RANK = 512
STEP = 4
TOK_DEV = 384
TOKENS = 12288
N_DP = 16
N_FSDP = 2


def draw_tokens(key, part):
    key = jax.random.fold_in(key, 11)
    key_base, key_rows, key_cols = jax.random.split(key, 3)
    row_scale = 10.0 ** jax.random.uniform(key_rows, (TOKENS, 1), jnp.float32, -0.5, 0.5)
    col_scale = 10.0 ** jax.random.uniform(key_cols, (1, D), jnp.float32, -0.5, 0.5)
    base = jax.random.truncated_normal(key_base, -4.0, 4.0, (TOKENS, D), jnp.float32)
    return (base * row_scale * col_scale).astype(jnp.bfloat16)


def block_scale(key, shape, cuts, smallest, top_value):
    loudness = 1.0
    for dim, shards_of in cuts:
        steps = jax.random.uniform(jax.random.fold_in(jax.random.fold_in(key, 6), dim), (shards_of,), jnp.float32, smallest / len(cuts), top_value / len(cuts))
        loudness = loudness * jnp.repeat(jnp.exp(steps), shape[dim] // shards_of).reshape((-1,) + (1,) * (len(shape) - 1 - dim))
    return loudness


def gaussian(key, extent, spread, limit, shards=(), held_as=jnp.bfloat16):
    values = jax.random.normal(key, extent, jnp.float32) * spread
    if len(shards) > 0:
        values = block_scale(key, extent, shards, -0.22, 0.18) * values
    return jnp.clip(values, min=-limit, max=limit).astype(held_as)


def setup_inputs(seed: int = 0) -> dict:
    seeds = jax.random.split(jax.random.key(seed), 8)
    return {
        "tokens": draw_tokens(jax.random.fold_in(seeds[7], 71), 0),
        "norm_gain": jnp.clip(1.0 + 0.18 * jax.random.normal(seeds[1], (D,), jnp.float32), 0.099609375, 1.8984375).astype(jnp.bfloat16),
        "key_weight": gaussian(seeds[2], (D, KV), D ** -0.5, 0.0625, ((0, 2),)),
        "key_cotangent": gaussian(seeds[3], (TOKENS, KV), (1.0 / TOKENS ** 0.5), 0.125, ((0, 32),)),
        "basis": gaussian(seeds[4], (KV, RANK), KV ** -0.5, 0.21875),
        "exp_avg": gaussian(seeds[5], (RANK, D), 0.5, 4.0, ((0, 16), (1, 2)), jnp.float32),
        "exp_avg_sq": jnp.clip(jnp.exp(math.log(2.0) - 2.3025851 * jax.random.uniform(seeds[6], (RANK, D), jnp.float32) ** block_scale(seeds[6], (RANK, D), ((0, 16), (1, 2)), -0.2, 0.2)), 0.2, 2.0),
    }


def reference(tokens, norm_gain, key_weight, key_cotangent, basis, exp_avg, exp_avg_sq):
    blocks = N_DP * N_FSDP
    token_blocks = tokens.reshape(blocks, TOK_DEV, D)
    grad_blocks = key_cotangent.reshape(blocks, TOK_DEV, KV)
    gain = norm_gain.astype(jnp.float32)

    def accumulate(total, pair):
        block, cotangent = pair
        values = block.astype(jnp.float32)
        scale = lax.rsqrt(lax.optimization_barrier(jnp.mean(values * values, axis=-1, keepdims=True)) + 1e-05)
        normed = (values * scale * gain).astype(jnp.bfloat16)
        keys = jnp.dot(normed, key_weight, preferred_element_type=jnp.float32).astype(jnp.bfloat16)
        projected = jnp.dot(cotangent, basis, preferred_element_type=jnp.float32).astype(jnp.bfloat16)
        total = total + jnp.dot(projected.T, normed, preferred_element_type=jnp.float32)
        return (total, keys)
    grad_t, keys = lax.scan(accumulate, jnp.zeros((RANK, D), jnp.float32), (token_blocks, grad_blocks))
    keys = keys.reshape(TOKENS, KV)
    new_exp_avg = 0.9 * exp_avg + 0.1 * grad_t
    new_exp_avg_sq = 0.95 * exp_avg_sq + 0.05 * grad_t * grad_t
    first = new_exp_avg / (1.0 - 0.9 ** STEP)
    second = new_exp_avg_sq / (1.0 - 0.95 ** STEP)
    normalized = (first / (jnp.sqrt(second) + 1e-08)).astype(jnp.bfloat16)
    update = (0.25 * jnp.dot(normalized.T, basis.T, preferred_element_type=jnp.float32)).astype(jnp.bfloat16)
    return (keys, new_exp_avg, new_exp_avg_sq, update)
```

```python
import functools

import jax
import jax.numpy as jnp
from jax import lax
from jax.experimental import pallas as pl
from jax.experimental.pallas import tpu as pltpu
from jax.sharding import PartitionSpec as P

STEP = 4
CHUNKS = 8
PIECES = 2
ROW_TILE = 16
MESH_ID = pl.DeviceIdType.MESH
BF16 = jnp.bfloat16
F32 = jnp.float32


def remote(src, dst, send_sem, recv_sem, to):
    return pltpu.make_async_remote_copy(
        src_ref=src, dst_ref=dst, send_sem=send_sem, recv_sem=recv_sem,
        device_id=to, device_id_type=MESH_ID,
    )


def kernel(
    n_dp, n_f,
    tok_hbm, gain_ref, w_hbm, cot_ref, basis_ref, m_ref, v_ref,
    keys_ref, m_out, v_out, whole_out,
    normed, w_all, proj, core_tx, core_rx, x_tx, x_rx, y_tx, y_rx, z_own, z_tx, z_rx,
    whole, acc,
    load_sem, core_s, core_r, x_s, x_r, y_s, y_r, z_s, z_r,
    gz_s, gz_r, gx_s, gx_r, gc_s, gc_r, w1_s, w1_r, w2_s, w2_r, w3_s, w3_r, out_sem,
):
    n_z = n_dp // 4
    dp = lax.axis_index("dp")
    y = lax.axis_index("fsdp")
    core = lax.rem(dp, 2)
    x = lax.rem(lax.div(dp, 2), 2)
    z = lax.div(dp, 4)
    other_core, other_x = 1 - core, 1 - x
    dev_core = (dp + 1 - 2 * core, y)
    dev_x = (dp + 2 - 4 * x, y)
    z_bit = lax.rem(z, 2)
    dev_pair = (dp + 4 - 8 * z_bit, y)

    def at_y(k):
        return lax.rem(y + k, n_f)

    def at_z(k):
        return lax.rem(z + k, n_z)

    def dev_z(zi):
        return (zi * 4 + x * 2 + core, y)

    d_f = w_hbm.shape[0]
    rows, d = normed.shape
    cw = d_f // CHUNKS
    r = proj.shape[3]
    quarter = d_f // 4
    piece = quarter // PIECES

    load_tok = pltpu.make_async_copy(tok_hbm, normed, load_sem.at[0])
    load_tok.start()

    barrier = pltpu.get_barrier_semaphore()
    peers = [dev_core, dev_x]
    peers += [(dp, at_y(k)) for k in range(1, n_f)]
    peers += [dev_z(at_z(k)) for k in range(1, n_z)]
    for peer in peers:
        pl.semaphore_signal(barrier, inc=1, device_id=peer, device_id_type=MESH_ID)
    pl.semaphore_wait(barrier, len(peers))

    my_q = core + 2 * z_bit
    pair_q = core + 2 * (1 - z_bit)

    def w_rows(q, p):
        return pl.ds(pl.multiple_of(q * quarter + p * piece, piece), piece)

    def w1(p, k):
        return remote(
            w_hbm.at[w_rows(my_q, p)], w_all.at[y, w_rows(my_q, p)],
            w1_s.at[p, k - 1], w1_r.at[p, k - 1], (dp, at_y(n_f - k)),
        )

    def w2(p, k, j):
        blk = w_all.at[at_y(k), w_rows(my_q, p)]
        return remote(blk, blk, w2_s.at[p, k - 1, j], w2_r.at[p, k - 1, j],
                      dev_pair if j == 0 else dev_core)

    def w3(p, k):
        blk = w_all.at[at_y(k), w_rows(pair_q, p)]
        return remote(blk, blk, w3_s.at[p, k - 1], w3_r.at[p, k - 1], dev_core)

    for p in range(PIECES):
        for k in range(1, n_f):
            w1(p, k).start()

    load_w = pltpu.make_async_copy(w_hbm, w_all.at[y], load_sem.at[1])
    load_w.start()

    projected = lax.dot_general(
        basis_ref[...], cot_ref[...], (((0,), (1,)), ((), ())), preferred_element_type=F32
    ).astype(BF16)
    proj[...] = projected.reshape(proj.shape)

    load_tok.wait()

    gain = gain_ref[...].astype(F32)

    @pl.loop(0, rows // ROW_TILE)
    def _(i):
        sl = pl.ds(pl.multiple_of(i * ROW_TILE, ROW_TILE), ROW_TILE)
        values = normed[sl, :].astype(F32)
        scale = lax.rsqrt(jnp.mean(values * values, axis=-1, keepdims=True) + 1e-05)
        normed[sl, :] = (values * scale * gain).astype(BF16)

    def cols(f, t):
        return pl.ds(pl.multiple_of(f * d_f + t * cw, cw), cw)

    def part(lhs, f, t):
        return jnp.dot(lhs, normed[:, cols(f, t)], preferred_element_type=F32)

    def core_copy(t):
        return remote(core_tx.at[t], core_rx.at[t], core_s.at[t], core_r.at[t], dev_core)

    def x_copy(t):
        return remote(x_tx.at[t], x_rx.at[t], x_s.at[t], x_r.at[t], dev_x)

    def y_copy(t, k):
        return remote(y_tx.at[t, k - 1], y_rx.at[t, k - 1], y_s.at[t, k - 1],
                      y_r.at[t, k - 1], (dp, at_y(k)))

    def z_copy(t, k):
        return remote(z_tx.at[t, at_z(k)], z_rx.at[t, k - 1], z_s.at[t, k - 1],
                      z_r.at[t, k - 1], dev_z(at_z(k)))

    def gz_send(t, k):
        blk = whole.at[t, z, x, core]
        return remote(blk, blk, gz_s.at[t, k - 1], gz_r.at[t, k - 1], dev_z(at_z(k)))

    def gx_send(t):
        blk = whole.at[t, :, x, core]
        return remote(blk, blk, gx_s.at[t], gx_r.at[t], dev_x)

    def gc_send(t):
        blk = whole.at[t, :, :, core]
        return remote(blk, blk, gc_s.at[t], gc_r.at[t], dev_core)

    def stage_core(t):
        lhs = proj[:, :, other_core].reshape(n_z * 2 * r, rows)
        for f in range(n_f):
            core_tx[t, f] = part(lhs, f, t).astype(BF16).reshape(core_tx.shape[2:])
        core_copy(t).start()

    def stage_x(t):
        core_copy(t).wait_recv()
        lhs = proj[:, other_x, core].reshape(n_z * r, rows)
        for f in range(n_f):
            mine = part(lhs, f, t).reshape(n_z, r, cw)
            x_tx[t, f] = (mine + core_rx[t, f, :, other_x].astype(F32)).astype(BF16)
        x_copy(t).start()

    def chip_sum(f, t):
        mine = part(proj[:, x, core].reshape(n_z * r, rows), f, t).reshape(n_z, r, cw)
        return mine + core_rx[t, f, :, x].astype(F32) + x_rx[t, f].astype(F32)

    def stage_y(t):
        x_copy(t).wait_recv()
        for k in range(1, n_f):
            y_tx[t, k - 1] = chip_sum(at_y(k), t).astype(BF16)
            y_copy(t, k).start()

    def stage_z(t):
        for k in range(1, n_f):
            y_copy(t, k).wait_recv()
        total = chip_sum(y, t)
        for k in range(1, n_f):
            total = total + y_rx[t, k - 1].astype(F32)
        z_own[t] = total
        z_tx[t] = total.astype(BF16)
        for k in range(1, n_z):
            z_copy(t, k).start()

    def stage_adam(t):
        for k in range(1, n_z):
            z_copy(t, k).wait_recv()
        grad = z_own[t, z]
        for k in range(1, n_z):
            grad = grad + z_rx[t, k - 1].astype(F32)
        sl = pl.ds(pl.multiple_of(t * cw, cw), cw)
        m = 0.9 * m_ref[:, sl] + 0.1 * grad
        v = 0.95 * v_ref[:, sl] + 0.05 * grad * grad
        m_out[:, sl] = m
        v_out[:, sl] = v
        first = m / (1.0 - 0.9**STEP)
        second = v / (1.0 - 0.95**STEP)
        whole[t, z, x, core] = (first / (jnp.sqrt(second) + 1e-08)).astype(BF16)
        for k in range(1, n_z):
            gz_send(t, k).start()

    def stage_gx(t):
        for k in range(1, n_z):
            gz_send(t, k).wait_recv()
        gx_send(t).start()

    def stage_gc(t):
        gx_send(t).wait_recv()
        gc_send(t).start()

    def keys_part(f, t):
        rhs = w_all[f, pl.ds(pl.multiple_of(t * cw, cw), cw), :]
        return jnp.dot(normed[:, cols(f, t)], rhs, preferred_element_type=F32)

    def w_forward(p):
        for k in range(1, n_f):
            w1(p, k).wait_recv()
            w2(p, k, 0).start()
            w2(p, k, 1).start()

    def w_last(p):
        for k in range(1, n_f):
            w2(p, k, 0).wait_recv()
            w3(p, k).start()

    load_w.wait()
    acc[...] = jnp.zeros_like(acc)
    stages = [stage_core, stage_x, stage_y, stage_z, stage_adam, stage_gx, stage_gc]
    w_steps = {4: [(w_forward, 0)], 6: [(w_forward, 1)], 9: [(w_last, 0)], 12: [(w_last, 1)]}

    @pl.loop(0, CHUNKS + len(stages) - 1)
    def _(s):
        for lag, stage in reversed(list(enumerate(stages))):
            @pl.when(jnp.logical_and(s >= lag, s < CHUNKS + lag))
            def _():
                stage(s - lag)

        @pl.when(s < CHUNKS)
        def _():
            acc[...] += keys_part(y, s)

        for at, calls in w_steps.items():
            @pl.when(s == at)
            def _():
                for call, p in calls:
                    call(p)

    for p in range(PIECES):
        for k in range(1, n_f):
            w2(p, k, 1).wait_recv()
            w3(p, k).wait_recv()

    for k in range(1, n_f):
        @pl.loop(0, CHUNKS)
        def _(t):
            acc[...] += keys_part(at_y(k), t)

    keys_ref[...] = acc[...].astype(BF16)

    def out_copy(t):
        return pltpu.make_async_copy(whole.at[t], whole_out.at[t], out_sem.at[t])

    @pl.loop(0, CHUNKS)
    def _(t):
        gc_send(t).wait_recv()
        out_copy(t).start()

    @pl.loop(0, CHUNKS)
    def _(t):
        core_copy(t).wait_send()
        x_copy(t).wait_send()
        for k in range(1, n_f):
            y_copy(t, k).wait_send()
        for k in range(1, n_z):
            z_copy(t, k).wait_send()
            gz_send(t, k).wait_send()
        gx_send(t).wait_send()
        gc_send(t).wait_send()
        out_copy(t).wait()

    for p in range(PIECES):
        for k in range(1, n_f):
            w1(p, k).wait_send()
            w2(p, k, 0).wait_send()
            w2(p, k, 1).wait_send()
            w3(p, k).wait_send()


def per_device(n_dp, n_f, tokens, norm_gain, key_weight, key_cotangent, basis, exp_avg, exp_avg_sq):
    rows, d = tokens.shape
    d_f, kv = key_weight.shape
    rank = basis.shape[1]
    r = exp_avg.shape[0]
    n_z = n_dp // 4
    cw = d_f // CHUNKS
    c = CHUNKS
    vm = pl.BlockSpec(memory_space=pltpu.VMEM)
    hbm = pl.BlockSpec(memory_space=pl.ANY)
    dma = pltpu.SemaphoreType.DMA
    keys, m_new, v_new, whole = pl.pallas_call(
        functools.partial(kernel, n_dp, n_f),
        out_shape=(
            jax.ShapeDtypeStruct((rows, kv), BF16),
            jax.ShapeDtypeStruct(exp_avg.shape, F32),
            jax.ShapeDtypeStruct(exp_avg.shape, F32),
            jax.ShapeDtypeStruct((c, n_z, 2, 2, r, cw), BF16),
        ),
        in_specs=[hbm, vm, hbm, vm, vm, vm, vm],
        out_specs=(vm, vm, vm, hbm),
        scratch_shapes=[
            pltpu.VMEM((rows, d), BF16),
            pltpu.VMEM((n_f, d_f, kv), BF16),
            pltpu.VMEM((n_z, 2, 2, r, rows), BF16),
            pltpu.VMEM((c, n_f, n_z, 2, r, cw), BF16),
            pltpu.VMEM((c, n_f, n_z, 2, r, cw), BF16),
            pltpu.VMEM((c, n_f, n_z, r, cw), BF16),
            pltpu.VMEM((c, n_f, n_z, r, cw), BF16),
            pltpu.VMEM((c, n_f - 1, n_z, r, cw), BF16),
            pltpu.VMEM((c, n_f - 1, n_z, r, cw), BF16),
            pltpu.VMEM((c, n_z, r, cw), F32),
            pltpu.VMEM((c, n_z, r, cw), BF16),
            pltpu.VMEM((c, n_z - 1, r, cw), BF16),
            pltpu.VMEM((c, n_z, 2, 2, r, cw), BF16),
            pltpu.VMEM((rows, kv), F32),
            dma((2,)),
            dma((c,)), dma((c,)),
            dma((c,)), dma((c,)),
            dma((c, n_f - 1)), dma((c, n_f - 1)),
            dma((c, n_z - 1)), dma((c, n_z - 1)),
            dma((c, n_z - 1)), dma((c, n_z - 1)),
            dma((c,)), dma((c,)),
            dma((c,)), dma((c,)),
            dma((PIECES, n_f - 1)), dma((PIECES, n_f - 1)),
            dma((PIECES, n_f - 1, 2)), dma((PIECES, n_f - 1, 2)),
            dma((PIECES, n_f - 1)), dma((PIECES, n_f - 1)),
            dma((c,)),
        ],
        compiler_params=pltpu.CompilerParams(
            collective_id=0, has_side_effects=True, vmem_limit_bytes=60 * 2**20
        ),
    )(tokens, norm_gain.reshape(1, d), key_weight, key_cotangent, basis, exp_avg, exp_avg_sq)
    back = lax.dot_general(
        whole.reshape(c, rank, cw), basis, (((1,), (1,)), ((), ())), preferred_element_type=F32
    )
    update = (0.25 * back).astype(BF16).reshape(d_f, kv)
    return keys, m_new, v_new, update


def solution(mesh):
    in_specs = (
        P(("dp", "fsdp"), None),
        P(),
        P("fsdp", None),
        P(("dp", "fsdp"), None),
        P(),
        P("dp", "fsdp"),
        P("dp", "fsdp"),
    )
    out_specs = (P(("dp", "fsdp"), None), P("dp", "fsdp"), P("dp", "fsdp"), P("fsdp", None))
    return jax.shard_map(
        functools.partial(per_device, mesh.shape["dp"], mesh.shape["fsdp"]),
        mesh=mesh, in_specs=in_specs, out_specs=out_specs, check_vma=False,
    )
```

```python
import functools

import jax
import jax.numpy as jnp
from jax import lax
from jax.experimental import pallas as pl
from jax.experimental.pallas import tpu as pltpu
from jax.sharding import PartitionSpec as P

STEP = 4
CHUNKS = 8
PIECES = 4
ROW_TILE = 16
MESH_ID = pl.DeviceIdType.MESH
BF16 = jnp.bfloat16
F32 = jnp.float32


def remote(src, dst, send_sem, recv_sem, to):
    return pltpu.make_async_remote_copy(
        src_ref=src, dst_ref=dst, send_sem=send_sem, recv_sem=recv_sem,
        device_id=to, device_id_type=MESH_ID,
    )


def kernel(
    n_dp, n_f,
    tok_hbm, gain_ref, w_hbm, cot_ref, basis_ref, m_ref, v_ref,
    keys_ref, m_out, v_out, update_out,
    normed, w_all, proj, core_tx, core_rx, x_tx, x_rx, y_tx, y_rx, ya_tx, ya_rx, xb_tx, xb_rx,
    z_own, z_tx, z_rx, whole, acc, u_buf,
    load_sem, core_s, core_r, x_s, x_r, y_s, y_r, z_s, z_r,
    gz_s, gz_r, gx_s, gx_r, gc_s, gc_r, w1_s, w1_r, w2_s, w2_r, w3_s, w3_r, out_sem,
):
    n_z = n_dp // 4
    dp = lax.axis_index("dp")
    y = lax.axis_index("fsdp")
    core = lax.rem(dp, 2)
    x = lax.rem(lax.div(dp, 2), 2)
    z = lax.div(dp, 4)
    other_core, other_x = 1 - core, 1 - x
    dev_core = (dp + 1 - 2 * core, y)
    dev_x = (dp + 2 - 4 * x, y)
    z_bit = lax.rem(z, 2)
    dev_pair = (dp + 4 - 8 * z_bit, y)

    def at_y(k):
        return lax.rem(y + k, n_f)

    def at_z(k):
        return lax.rem(z + k, n_z)

    def dev_z(zi):
        return (zi * 4 + x * 2 + core, y)

    d_f = w_hbm.shape[0]
    rows, d = normed.shape
    cw = d_f // CHUNKS
    r = proj.shape[3]
    quarter = d_f // 4
    piece = quarter // PIECES

    load_tok = pltpu.make_async_copy(tok_hbm, normed, load_sem.at[0])
    load_tok.start()

    barrier = pltpu.get_barrier_semaphore()
    peers = [dev_core, dev_x]
    peers += [(dp, at_y(k)) for k in range(1, n_f)]
    peers += [dev_z(at_z(k)) for k in range(1, n_z)]
    for peer in peers:
        pl.semaphore_signal(barrier, inc=1, device_id=peer, device_id_type=MESH_ID)
    pl.semaphore_wait(barrier, len(peers))

    my_q = core + 2 * z_bit
    pair_q = core + 2 * (1 - z_bit)

    def w_rows(q, p):
        return pl.ds(pl.multiple_of(q * quarter + p * piece, piece), piece)

    def w1(p, k):
        return remote(
            w_hbm.at[w_rows(my_q, p)], w_all.at[y, w_rows(my_q, p)],
            w1_s.at[p, k - 1], w1_r.at[p, k - 1], (dp, at_y(n_f - k)),
        )

    def w2(p, k, j):
        blk = w_all.at[at_y(k), w_rows(my_q, p)]
        return remote(blk, blk, w2_s.at[p, k - 1, j], w2_r.at[p, k - 1, j],
                      dev_pair if j == 0 else dev_core)

    def w3(p, k):
        blk = w_all.at[at_y(k), w_rows(pair_q, p)]
        return remote(blk, blk, w3_s.at[p, k - 1], w3_r.at[p, k - 1], dev_core)

    def w_begin(p):
        for k in range(1, n_f):
            w1(p, k).start()

    w_begin(0)
    w_begin(1)

    load_w = pltpu.make_async_copy(w_hbm, w_all.at[y], load_sem.at[1])
    load_w.start()

    projected = lax.dot_general(
        basis_ref[...], cot_ref[...], (((0,), (1,)), ((), ())), preferred_element_type=F32
    ).astype(BF16)
    proj[...] = projected.reshape(proj.shape)

    load_tok.wait()

    gain = gain_ref[...].astype(F32)

    @pl.loop(0, rows // ROW_TILE)
    def _(i):
        sl = pl.ds(pl.multiple_of(i * ROW_TILE, ROW_TILE), ROW_TILE)
        values = normed[sl, :].astype(F32)
        scale = lax.rsqrt(jnp.mean(values * values, axis=-1, keepdims=True) + 1e-05)
        normed[sl, :] = (values * scale * gain).astype(BF16)

    def cols(f, t):
        return pl.ds(pl.multiple_of(f * d_f + t * cw, cw), cw)

    def part(lhs, f, t):
        return jnp.dot(lhs, normed[:, cols(f, t)], preferred_element_type=F32)

    def core_copy(t):
        return remote(core_tx.at[t], core_rx.at[t], core_s.at[t], core_r.at[t], dev_core)

    def x_copy(t):
        h = lax.div(t, 2)
        return remote(x_tx.at[h], x_rx.at[h], x_s.at[t], x_r.at[t], dev_x)

    def y_copy(t, k):
        h = lax.div(t, 2)
        return remote(y_tx.at[h, k - 1], y_rx.at[h, k - 1], y_s.at[t, k - 1],
                      y_r.at[t, k - 1], (dp, at_y(k)))

    def ya_copy(t, k):
        h = lax.div(t, 2)
        return remote(ya_tx.at[h, k - 1], ya_rx.at[h, k - 1], y_s.at[t, k - 1],
                      y_r.at[t, k - 1], (dp, at_y(k)))

    def xb_copy(t):
        h = lax.div(t, 2)
        return remote(xb_tx.at[h], xb_rx.at[h], x_s.at[t], x_r.at[t], dev_x)

    def z_copy(t, k):
        return remote(z_tx.at[t, at_z(k)], z_rx.at[t, k - 1], z_s.at[t, k - 1],
                      z_r.at[t, k - 1], dev_z(at_z(k)))

    def gz_send(t, k):
        blk = whole.at[t, z, x, core]
        return remote(blk, blk, gz_s.at[t, k - 1], gz_r.at[t, k - 1], dev_z(at_z(k)))

    def gx_send(t):
        blk = whole.at[t, :, x, core]
        return remote(blk, blk, gx_s.at[t], gx_r.at[t], dev_x)

    def gc_send(t):
        blk = whole.at[t, :, :, core]
        return remote(blk, blk, gc_s.at[t], gc_r.at[t], dev_core)

    def stage_core(t):
        lhs = proj[:, :, other_core].reshape(n_z * 2 * r, rows)
        for f in range(n_f):
            core_tx[t, f] = part(lhs, f, t).astype(BF16).reshape(core_tx.shape[2:])
        core_copy(t).start()

    def core_sum(f, t, xi):
        mine = part(proj[:, xi, core].reshape(n_z * r, rows), f, t).reshape(n_z, r, cw)
        return mine + core_rx[t, f, :, xi].astype(F32)

    def even_first(t):
        core_copy(t).wait_recv()
        for f in range(n_f):
            x_tx[lax.div(t, 2), f] = core_sum(f, t, other_x).astype(BF16)
        x_copy(t).start()

    def even_second(t):
        h = lax.div(t, 2)
        x_copy(t).wait_recv()
        for k in range(1, n_f):
            f = at_y(k)
            y_tx[h, k - 1] = (core_sum(f, t, x) + x_rx[h, f].astype(F32)).astype(BF16)
            y_copy(t, k).start()

    def send_z(t, total):
        z_own[t] = total
        z_tx[t] = total.astype(BF16)
        for k in range(1, n_z):
            z_copy(t, k).start()

    def even_third(t):
        h = lax.div(t, 2)
        for k in range(1, n_f):
            y_copy(t, k).wait_recv()
        total = core_sum(y, t, x) + x_rx[h, y].astype(F32)
        for k in range(1, n_f):
            total = total + y_rx[h, k - 1].astype(F32)
        send_z(t, total)

    def odd_first(t):
        h = lax.div(t, 2)
        core_copy(t).wait_recv()
        lhs = proj[:, :, core].reshape(n_z * 2 * r, rows)
        for k in range(1, n_f):
            f = at_y(k)
            mine = part(lhs, f, t).reshape(n_z, 2, r, cw)
            ya_tx[h, k - 1] = (mine + core_rx[t, f].astype(F32)).astype(BF16)
            ya_copy(t, k).start()

    def odd_sum(t, xi):
        total = core_sum(y, t, xi)
        for k in range(1, n_f):
            total = total + ya_rx[lax.div(t, 2), k - 1, :, xi].astype(F32)
        return total

    def odd_second(t):
        for k in range(1, n_f):
            ya_copy(t, k).wait_recv()
        xb_tx[lax.div(t, 2)] = odd_sum(t, other_x).astype(BF16)
        xb_copy(t).start()

    def odd_third(t):
        xb_copy(t).wait_recv()
        send_z(t, odd_sum(t, x) + xb_rx[lax.div(t, 2)].astype(F32))

    def stage_adam(t):
        for k in range(1, n_z):
            z_copy(t, k).wait_recv()
        grad = z_own[t, z]
        for k in range(1, n_z):
            grad = grad + z_rx[t, k - 1].astype(F32)
        sl = pl.ds(pl.multiple_of(t * cw, cw), cw)
        m = 0.9 * m_ref[:, sl] + 0.1 * grad
        v = 0.95 * v_ref[:, sl] + 0.05 * grad * grad
        m_out[:, sl] = m
        v_out[:, sl] = v
        first = m / (1.0 - 0.9**STEP)
        second = v / (1.0 - 0.95**STEP)
        whole[t, z, x, core] = (first / (jnp.sqrt(second) + 1e-08)).astype(BF16)
        for k in range(1, n_z):
            gz_send(t, k).start()

    def stage_gx(t):
        for k in range(1, n_z):
            gz_send(t, k).wait_recv()
        gx_send(t).start()

    def stage_gc(t):
        gx_send(t).wait_recv()
        gc_send(t).start()

    def update_copy(t):
        return pltpu.make_async_copy(
            u_buf.at[lax.rem(t, 2)],
            update_out.at[pl.ds(pl.multiple_of(t * cw, cw), cw), :],
            out_sem.at[lax.rem(t, 2)],
        )

    def stage_update(t):
        gc_send(t).wait_recv()

        @pl.when(t >= 2)
        def _():
            update_copy(t - 2).wait()

        back = lax.dot_general(
            whole[t].reshape(n_z * 4 * r, cw), basis_ref[...], (((0,), (1,)), ((), ())),
            preferred_element_type=F32,
        )
        u_buf[lax.rem(t, 2)] = (0.25 * back).astype(BF16)
        update_copy(t).start()

    kv = acc.shape[1]
    n_tile = 256
    n_cols = kv // n_tile

    def keys_part(f, n):
        sl = pl.ds(pl.multiple_of(n * n_tile, n_tile), n_tile)
        lhs = normed[:, pl.ds(pl.multiple_of(f * d_f, d_f), d_f)]
        return sl, jnp.dot(lhs, w_all[f, :, sl], preferred_element_type=F32)

    def stage_keys(n):
        sl, own = keys_part(y, n)
        acc[:, sl] = own

    def w_forward(p):
        for k in range(1, n_f):
            w1(p, k).wait_recv()
            w2(p, k, 0).start()
            w2(p, k, 1).start()

    def w_last(p):
        for k in range(1, n_f):
            w2(p, k, 0).wait_recv()
            w3(p, k).start()

    load_w.wait()
    stages = [
        (0, stage_core, stage_core), (1, even_first, odd_first), (3, even_second, odd_second),
        (5, even_third, odd_third), (7, stage_adam, stage_adam), (9, stage_gx, stage_gx),
        (11, stage_gc, stage_gc), (13, stage_update, stage_update),
    ]
    w_steps = {
        5: (w_forward, 0), 7: (w_forward, 1), 12: (w_forward, 2), 14: (w_forward, 3),
        8: (w_last, 0), 10: (w_last, 1), 15: (w_last, 2), 17: (w_last, 3),
    }
    w_starts = {8: 2, 10: 3}

    def run_if(cond, stage, t):
        @pl.when(cond)
        def _():
            stage(t)

    @pl.loop(0, CHUNKS + 13)
    def _(s):
        for at, p in w_starts.items():
            run_if(s == at, w_begin, p)
        for lag, even, odd in stages:
            t = s - lag
            live = jnp.logical_and(t >= 0, t < CHUNKS)
            if even is odd:
                run_if(live, even, t)
            else:
                run_if(jnp.logical_and(live, lax.rem(s, 2) == lag % 2), even, t)
                run_if(jnp.logical_and(live, lax.rem(s, 2) != lag % 2), odd, t)
            if lag == 1:
                run_if(jnp.logical_and(s >= CHUNKS + 1, s < CHUNKS + 1 + n_cols),
                       stage_keys, s - CHUNKS - 1)
        for at, (call, p) in w_steps.items():
            run_if(s == at, call, p)

    for p in range(PIECES):
        for k in range(1, n_f):
            w2(p, k, 1).wait_recv()
            w3(p, k).wait_recv()

    for k in range(1, n_f):
        @pl.loop(0, n_cols)
        def _(n):
            sl, term = keys_part(at_y(k), n)
            acc[:, sl] += term

    keys_ref[...] = acc[...].astype(BF16)
    update_copy(CHUNKS - 2).wait()
    update_copy(CHUNKS - 1).wait()

    @pl.loop(0, CHUNKS)
    def _(t):
        core_copy(t).wait_send()
        run_if(lax.rem(t, 2) == 0, lambda u: x_copy(u).wait_send(), t)
        run_if(lax.rem(t, 2) == 1, lambda u: xb_copy(u).wait_send(), t)
        for k in range(1, n_f):
            run_if(lax.rem(t, 2) == 0, lambda u: y_copy(u, k).wait_send(), t)
            run_if(lax.rem(t, 2) == 1, lambda u: ya_copy(u, k).wait_send(), t)
        for k in range(1, n_z):
            z_copy(t, k).wait_send()
            gz_send(t, k).wait_send()
        gx_send(t).wait_send()
        gc_send(t).wait_send()

    for p in range(PIECES):
        for k in range(1, n_f):
            w1(p, k).wait_send()
            w2(p, k, 0).wait_send()
            w2(p, k, 1).wait_send()
            w3(p, k).wait_send()


def per_device(n_dp, n_f, tokens, norm_gain, key_weight, key_cotangent, basis, exp_avg, exp_avg_sq):
    rows, d = tokens.shape
    d_f, kv = key_weight.shape
    rank = basis.shape[1]
    r = exp_avg.shape[0]
    n_z = n_dp // 4
    cw = d_f // CHUNKS
    c = CHUNKS
    vm = pl.BlockSpec(memory_space=pltpu.VMEM)
    hbm = pl.BlockSpec(memory_space=pl.ANY)
    dma = pltpu.SemaphoreType.DMA
    return pl.pallas_call(
        functools.partial(kernel, n_dp, n_f),
        out_shape=(
            jax.ShapeDtypeStruct((rows, kv), BF16),
            jax.ShapeDtypeStruct(exp_avg.shape, F32),
            jax.ShapeDtypeStruct(exp_avg.shape, F32),
            jax.ShapeDtypeStruct((d_f, kv), BF16),
        ),
        in_specs=[hbm, vm, hbm, vm, vm, vm, vm],
        out_specs=(vm, vm, vm, hbm),
        scratch_shapes=[
            pltpu.VMEM((rows, d), BF16),
            pltpu.VMEM((n_f, d_f, kv), BF16),
            pltpu.VMEM((n_z, 2, 2, r, rows), BF16),
            pltpu.VMEM((c, n_f, n_z, 2, r, cw), BF16),
            pltpu.VMEM((c, n_f, n_z, 2, r, cw), BF16),
            pltpu.VMEM((c // 2, n_f, n_z, r, cw), BF16),
            pltpu.VMEM((c // 2, n_f, n_z, r, cw), BF16),
            pltpu.VMEM((c // 2, n_f - 1, n_z, r, cw), BF16),
            pltpu.VMEM((c // 2, n_f - 1, n_z, r, cw), BF16),
            pltpu.VMEM((c // 2, n_f - 1, n_z, 2, r, cw), BF16),
            pltpu.VMEM((c // 2, n_f - 1, n_z, 2, r, cw), BF16),
            pltpu.VMEM((c // 2, n_z, r, cw), BF16),
            pltpu.VMEM((c // 2, n_z, r, cw), BF16),
            pltpu.VMEM((c, n_z, r, cw), F32),
            pltpu.VMEM((c, n_z, r, cw), BF16),
            pltpu.VMEM((c, n_z - 1, r, cw), BF16),
            pltpu.VMEM((c, n_z, 2, 2, r, cw), BF16),
            pltpu.VMEM((rows, kv), F32),
            pltpu.VMEM((2, cw, kv), BF16),
            dma((2,)),
            dma((c,)), dma((c,)),
            dma((c,)), dma((c,)),
            dma((c, n_f - 1)), dma((c, n_f - 1)),
            dma((c, n_z - 1)), dma((c, n_z - 1)),
            dma((c, n_z - 1)), dma((c, n_z - 1)),
            dma((c,)), dma((c,)),
            dma((c,)), dma((c,)),
            dma((PIECES, n_f - 1)), dma((PIECES, n_f - 1)),
            dma((PIECES, n_f - 1, 2)), dma((PIECES, n_f - 1, 2)),
            dma((PIECES, n_f - 1)), dma((PIECES, n_f - 1)),
            dma((2,)),
        ],
        compiler_params=pltpu.CompilerParams(
            collective_id=0, has_side_effects=True, vmem_limit_bytes=60 * 2**20
        ),
    )(tokens, norm_gain.reshape(1, d), key_weight, key_cotangent, basis, exp_avg, exp_avg_sq)


def solution(mesh):
    in_specs = (
        P(("dp", "fsdp"), None),
        P(),
        P("fsdp", None),
        P(("dp", "fsdp"), None),
        P(),
        P("dp", "fsdp"),
        P("dp", "fsdp"),
    )
    out_specs = (P(("dp", "fsdp"), None), P("dp", "fsdp"), P("dp", "fsdp"), P("fsdp", None))
    return jax.shard_map(
        functools.partial(per_device, mesh.shape["dp"], mesh.shape["fsdp"]),
        mesh=mesh, in_specs=in_specs, out_specs=out_specs, check_vma=False,
    )
```

```python
import functools

import jax
import jax.numpy as jnp
from jax import lax
from jax.experimental import pallas as pl
from jax.experimental.pallas import tpu as pltpu
from jax.sharding import PartitionSpec as P

STEP = 4
CHUNKS = 8
PIECES = 4
ROW_TILE = 16
MESH_ID = pl.DeviceIdType.MESH
BF16 = jnp.bfloat16
F32 = jnp.float32


def remote(src, dst, send_sem, recv_sem, to):
    return pltpu.make_async_remote_copy(
        src_ref=src, dst_ref=dst, send_sem=send_sem, recv_sem=recv_sem,
        device_id=to, device_id_type=MESH_ID,
    )


def kernel(
    n_dp, n_f,
    tok_hbm, gain_ref, w_hbm, cot_ref, basis_ref, m_ref, v_ref,
    keys_ref, m_out, v_out, update_out,
    normed, w_all, whole_rank, proj, core_tx, core_rx, x_tx, x_rx, y_tx, y_rx, ya_tx, ya_rx, xb_tx, xb_rx,
    own, z_tx, z_rx, whole, acc, u_buf,
    load_sem, core_s, core_r, x_s, x_r, y_s, y_r, z_s, z_r,
    gz_s, gz_r, gx_s, gx_r, gc_s, gc_r, w1_s, w1_r, w2_s, w2_r, w3_s, w3_r, out_sem,
):
    n_z = n_dp // 4
    dp = lax.axis_index("dp")
    y = lax.axis_index("fsdp")
    core = lax.rem(dp, 2)
    x = lax.rem(lax.div(dp, 2), 2)
    z = lax.div(dp, 4)
    other_core, other_x = 1 - core, 1 - x
    dev_core = (dp + 1 - 2 * core, y)
    dev_x = (dp + 2 - 4 * x, y)
    z_bit = lax.rem(z, 2)
    dev_pair = (dp + 4 - 8 * z_bit, y)

    def at_y(k):
        return lax.rem(y + k, n_f)

    def at_z(k):
        return lax.rem(z + k, n_z)

    def dev_z(zi):
        return (zi * 4 + x * 2 + core, y)

    d_f = w_hbm.shape[0]
    rows, d = normed.shape
    cw = d_f // CHUNKS
    r = whole_rank.shape[3]
    quarter = d_f // 4
    piece = quarter // PIECES

    load_tok = pltpu.make_async_copy(tok_hbm, normed, load_sem.at[0])
    load_tok.start()

    barrier = pltpu.get_barrier_semaphore()
    peers = [dev_core, dev_x]
    peers += [(dp, at_y(k)) for k in range(1, n_f)]
    peers += [dev_z(at_z(k)) for k in range(1, n_z)]
    for peer in peers:
        pl.semaphore_signal(barrier, inc=1, device_id=peer, device_id_type=MESH_ID)
    pl.semaphore_wait(barrier, len(peers))

    my_q = core + 2 * z_bit
    pair_q = core + 2 * (1 - z_bit)

    def w_rows(q, p):
        return pl.ds(pl.multiple_of(q * quarter + p * piece, piece), piece)

    def w1(p, k):
        return remote(
            w_hbm.at[w_rows(my_q, p)], w_all.at[y, w_rows(my_q, p)],
            w1_s.at[p, k - 1], w1_r.at[p, k - 1], (dp, at_y(n_f - k)),
        )

    def w2(p, k, j):
        blk = w_all.at[at_y(k), w_rows(my_q, p)]
        return remote(blk, blk, w2_s.at[p, k - 1, j], w2_r.at[p, k - 1, j],
                      dev_pair if j == 0 else dev_core)

    def w3(p, k):
        blk = w_all.at[at_y(k), w_rows(pair_q, p)]
        return remote(blk, blk, w3_s.at[p, k - 1], w3_r.at[p, k - 1], dev_core)

    def w_begin(p):
        for k in range(1, n_f):
            w1(p, k).start()

    w_begin(0)
    w_begin(1)

    load_w = pltpu.make_async_copy(w_hbm, w_all.at[y], load_sem.at[1])
    load_w.start()

    projected = lax.dot_general(
        basis_ref[...], cot_ref[...], (((0,), (1,)), ((), ())), preferred_element_type=F32
    ).astype(BF16)
    whole_rank[...] = projected.reshape(whole_rank.shape)
    for i, c_i in enumerate((core, other_core)):
        for j, x_j in enumerate((x, other_x)):
            proj[i, j] = whole_rank[:, x_j, c_i]

    load_tok.wait()

    gain = gain_ref[...].astype(F32).reshape(1, d)

    @pl.loop(0, rows // ROW_TILE)
    def _(i):
        sl = pl.ds(pl.multiple_of(i * ROW_TILE, ROW_TILE), ROW_TILE)
        values = normed[sl, :].astype(F32)
        scale = lax.rsqrt(jnp.mean(values * values, axis=-1, keepdims=True) + 1e-05)
        normed[sl, :] = (values * scale * gain).astype(BF16)

    def cols(f, t):
        return pl.ds(pl.multiple_of(f * d_f + t * cw, cw), cw)

    def core_copy(t):
        return remote(core_tx.at[t], core_rx.at[t], core_s.at[t], core_r.at[t], dev_core)

    def x_copy(t):
        h = lax.div(t, 2)
        return remote(x_tx.at[h], x_rx.at[h], x_s.at[t], x_r.at[t], dev_x)

    def y_copy(t, k):
        h = lax.div(t, 2)
        return remote(y_tx.at[h, k - 1], y_rx.at[h, k - 1], y_s.at[t, k - 1],
                      y_r.at[t, k - 1], (dp, at_y(k)))

    def ya_copy(t, k):
        h = lax.div(t, 2)
        return remote(ya_tx.at[h, k - 1], ya_rx.at[h, k - 1], y_s.at[t, k - 1],
                      y_r.at[t, k - 1], (dp, at_y(k)))

    def xb_copy(t):
        h = lax.div(t, 2)
        return remote(xb_tx.at[h], xb_rx.at[h], x_s.at[t], x_r.at[t], dev_x)

    def z_copy(t, k):
        return remote(z_tx.at[t, at_z(k)], z_rx.at[t, k - 1], z_s.at[t, k - 1],
                      z_r.at[t, k - 1], dev_z(at_z(k)))

    def gz_send(t, k):
        blk = whole.at[t, z, x, core]
        return remote(blk, blk, gz_s.at[t, k - 1], gz_r.at[t, k - 1], dev_z(at_z(k)))

    def gx_send(t):
        blk = whole.at[t, :, x, core]
        return remote(blk, blk, gx_s.at[t], gx_r.at[t], dev_x)

    def gc_send(t):
        blk = whole.at[t, :, :, core]
        return remote(blk, blk, gc_s.at[t], gc_r.at[t], dev_core)

    def stage_core(t):
        lhs = proj[...].reshape(4 * n_z * r, rows)
        half = 2 * n_z * r
        for k in range(n_f):
            term = jnp.dot(lhs, normed[:, cols(at_y(k), t)], preferred_element_type=F32)
            own[t, k] = term[:half].reshape(2, n_z, r, cw)
            core_tx[t, k] = term[half:].astype(BF16).reshape(2, n_z, r, cw)
        core_copy(t).start()

    def core_sum(t, k, xi):
        return own[t, k, xi] + core_rx[t, k, xi].astype(F32)

    def even_first(t):
        core_copy(t).wait_recv()
        for k in range(n_f):
            x_tx[lax.div(t, 2), k] = core_sum(t, k, 1).astype(BF16)
        x_copy(t).start()

    def even_second(t):
        h = lax.div(t, 2)
        x_copy(t).wait_recv()
        for k in range(1, n_f):
            y_tx[h, k - 1] = (core_sum(t, k, 0) + x_rx[h, k].astype(F32)).astype(BF16)
            y_copy(t, k).start()

    def send_z(t, total):
        own[t, 0, 0] = total
        z_tx[t] = total.astype(BF16)
        for k in range(1, n_z):
            z_copy(t, k).start()

    def even_third(t):
        h = lax.div(t, 2)
        for k in range(1, n_f):
            y_copy(t, k).wait_recv()
        total = core_sum(t, 0, 0) + x_rx[h, 0].astype(F32)
        for k in range(1, n_f):
            total = total + y_rx[h, k - 1].astype(F32)
        send_z(t, total)

    def odd_first(t):
        h = lax.div(t, 2)
        core_copy(t).wait_recv()
        for k in range(1, n_f):
            for xi in range(2):
                ya_tx[h, k - 1, xi] = core_sum(t, k, xi).astype(BF16)
            ya_copy(t, k).start()

    def odd_sum(t, xi):
        total = core_sum(t, 0, xi)
        for k in range(1, n_f):
            total = total + ya_rx[lax.div(t, 2), k - 1, xi].astype(F32)
        return total

    def odd_second(t):
        for k in range(1, n_f):
            ya_copy(t, k).wait_recv()
        xb_tx[lax.div(t, 2)] = odd_sum(t, 1).astype(BF16)
        xb_copy(t).start()

    def odd_third(t):
        xb_copy(t).wait_recv()
        send_z(t, odd_sum(t, 0) + xb_rx[lax.div(t, 2)].astype(F32))

    def stage_adam(t):
        for k in range(1, n_z):
            z_copy(t, k).wait_recv()
        grad = own[t, 0, 0, z]
        for k in range(1, n_z):
            grad = grad + z_rx[t, k - 1].astype(F32)
        sl = pl.ds(pl.multiple_of(t * cw, cw), cw)
        m = 0.9 * m_ref[:, sl] + 0.1 * grad
        v = 0.95 * v_ref[:, sl] + 0.05 * grad * grad
        m_out[:, sl] = m
        v_out[:, sl] = v
        first = m / (1.0 - 0.9**STEP)
        second = v / (1.0 - 0.95**STEP)
        whole[t, z, x, core] = (first / (jnp.sqrt(second) + 1e-08)).astype(BF16)
        for k in range(1, n_z):
            gz_send(t, k).start()

    def stage_gx(t):
        for k in range(1, n_z):
            gz_send(t, k).wait_recv()
        gx_send(t).start()

    def stage_gc(t):
        gx_send(t).wait_recv()
        gc_send(t).start()

    def update_copy(t):
        return pltpu.make_async_copy(
            u_buf.at[lax.rem(t, 2)],
            update_out.at[pl.ds(pl.multiple_of(t * cw, cw), cw), :],
            out_sem.at[lax.rem(t, 2)],
        )

    def stage_update(t):
        gc_send(t).wait_recv()

        @pl.when(t >= 2)
        def _():
            update_copy(t - 2).wait()

        back = lax.dot_general(
            whole[t].reshape(n_z * 4 * r, cw), basis_ref[...], (((0,), (1,)), ((), ())),
            preferred_element_type=F32,
        )
        u_buf[lax.rem(t, 2)] = (0.25 * back).astype(BF16)
        update_copy(t).start()

    kv = acc.shape[1]
    n_tile = 256
    n_cols = kv // n_tile

    def keys_part(f, n):
        sl = pl.ds(pl.multiple_of(n * n_tile, n_tile), n_tile)
        lhs = normed[:, pl.ds(pl.multiple_of(f * d_f, d_f), d_f)]
        return sl, jnp.dot(lhs, w_all[f, :, sl], preferred_element_type=F32)

    def stage_keys(n):
        sl, own = keys_part(y, n)
        acc[:, sl] = own

    def w_forward(p):
        for k in range(1, n_f):
            w1(p, k).wait_recv()
            w2(p, k, 0).start()
            w2(p, k, 1).start()

    def w_last(p):
        for k in range(1, n_f):
            w2(p, k, 0).wait_recv()
            w3(p, k).start()

    load_w.wait()
    stages = [
        (0, stage_core, stage_core), (1, even_first, odd_first), (3, even_second, odd_second),
        (5, even_third, odd_third), (7, stage_adam, stage_adam), (9, stage_gx, stage_gx),
        (11, stage_gc, stage_gc), (13, stage_update, stage_update),
    ]
    w_steps = {
        5: (w_forward, 0), 7: (w_forward, 1), 12: (w_forward, 2), 14: (w_forward, 3),
        8: (w_last, 0), 10: (w_last, 1), 15: (w_last, 2), 17: (w_last, 3),
    }
    w_starts = {8: 2, 10: 3}

    def run_if(cond, stage, t):
        @pl.when(cond)
        def _():
            stage(t)

    @pl.loop(0, CHUNKS + 13)
    def _(s):
        for at, p in w_starts.items():
            run_if(s == at, w_begin, p)
        for lag, even, odd in stages:
            t = s - lag
            live = jnp.logical_and(t >= 0, t < CHUNKS)
            if even is odd:
                run_if(live, even, t)
            else:
                run_if(jnp.logical_and(live, lax.rem(s, 2) == lag % 2), even, t)
                run_if(jnp.logical_and(live, lax.rem(s, 2) != lag % 2), odd, t)
            if lag == 1:
                run_if(jnp.logical_and(s >= CHUNKS + 1, s < CHUNKS + 1 + n_cols),
                       stage_keys, s - CHUNKS - 1)
        for at, (call, p) in w_steps.items():
            run_if(s == at, call, p)

    for p in range(PIECES):
        for k in range(1, n_f):
            w2(p, k, 1).wait_recv()
            w3(p, k).wait_recv()

    for k in range(1, n_f):
        @pl.loop(0, n_cols)
        def _(n):
            sl, term = keys_part(at_y(k), n)
            acc[:, sl] += term

    keys_ref[...] = acc[...].astype(BF16)
    update_copy(CHUNKS - 2).wait()
    update_copy(CHUNKS - 1).wait()

    @pl.loop(0, CHUNKS)
    def _(t):
        core_copy(t).wait_send()
        run_if(lax.rem(t, 2) == 0, lambda u: x_copy(u).wait_send(), t)
        run_if(lax.rem(t, 2) == 1, lambda u: xb_copy(u).wait_send(), t)
        for k in range(1, n_f):
            run_if(lax.rem(t, 2) == 0, lambda u: y_copy(u, k).wait_send(), t)
            run_if(lax.rem(t, 2) == 1, lambda u: ya_copy(u, k).wait_send(), t)
        for k in range(1, n_z):
            z_copy(t, k).wait_send()
            gz_send(t, k).wait_send()
        gx_send(t).wait_send()
        gc_send(t).wait_send()

    for p in range(PIECES):
        for k in range(1, n_f):
            w1(p, k).wait_send()
            w2(p, k, 0).wait_send()
            w2(p, k, 1).wait_send()
            w3(p, k).wait_send()


def per_device(n_dp, n_f, tokens, norm_gain, key_weight, key_cotangent, basis, exp_avg, exp_avg_sq):
    rows, d = tokens.shape
    d_f, kv = key_weight.shape
    rank = basis.shape[1]
    r = exp_avg.shape[0]
    n_z = n_dp // 4
    cw = d_f // CHUNKS
    c = CHUNKS
    vm = pl.BlockSpec(memory_space=pltpu.VMEM)
    hbm = pl.BlockSpec(memory_space=pl.ANY)
    dma = pltpu.SemaphoreType.DMA
    return pl.pallas_call(
        functools.partial(kernel, n_dp, n_f),
        out_shape=(
            jax.ShapeDtypeStruct((rows, kv), BF16),
            jax.ShapeDtypeStruct(exp_avg.shape, F32),
            jax.ShapeDtypeStruct(exp_avg.shape, F32),
            jax.ShapeDtypeStruct((d_f, kv), BF16),
        ),
        in_specs=[hbm, vm, hbm, vm, vm, vm, vm],
        out_specs=(vm, vm, vm, hbm),
        scratch_shapes=[
            pltpu.VMEM((rows, d), BF16),
            pltpu.VMEM((n_f, d_f, kv), BF16),
            pltpu.VMEM((n_z, 2, 2, r, rows), BF16),
            pltpu.VMEM((2, 2, n_z, r, rows), BF16),
            pltpu.VMEM((c, n_f, 2, n_z, r, cw), BF16),
            pltpu.VMEM((c, n_f, 2, n_z, r, cw), BF16),
            pltpu.VMEM((c // 2, n_f, n_z, r, cw), BF16),
            pltpu.VMEM((c // 2, n_f, n_z, r, cw), BF16),
            pltpu.VMEM((c // 2, n_f - 1, n_z, r, cw), BF16),
            pltpu.VMEM((c // 2, n_f - 1, n_z, r, cw), BF16),
            pltpu.VMEM((c // 2, n_f - 1, 2, n_z, r, cw), BF16),
            pltpu.VMEM((c // 2, n_f - 1, 2, n_z, r, cw), BF16),
            pltpu.VMEM((c // 2, n_z, r, cw), BF16),
            pltpu.VMEM((c // 2, n_z, r, cw), BF16),
            pltpu.VMEM((c, n_f, 2, n_z, r, cw), F32),
            pltpu.VMEM((c, n_z, r, cw), BF16),
            pltpu.VMEM((c, n_z - 1, r, cw), BF16),
            pltpu.VMEM((c, n_z, 2, 2, r, cw), BF16),
            pltpu.VMEM((rows, kv), F32),
            pltpu.VMEM((2, cw, kv), BF16),
            dma((2,)),
            dma((c,)), dma((c,)),
            dma((c,)), dma((c,)),
            dma((c, n_f - 1)), dma((c, n_f - 1)),
            dma((c, n_z - 1)), dma((c, n_z - 1)),
            dma((c, n_z - 1)), dma((c, n_z - 1)),
            dma((c,)), dma((c,)),
            dma((c,)), dma((c,)),
            dma((PIECES, n_f - 1)), dma((PIECES, n_f - 1)),
            dma((PIECES, n_f - 1, 2)), dma((PIECES, n_f - 1, 2)),
            dma((PIECES, n_f - 1)), dma((PIECES, n_f - 1)),
            dma((2,)),
        ],
        compiler_params=pltpu.CompilerParams(
            collective_id=0, has_side_effects=True, vmem_limit_bytes=60 * 2**20
        ),
    )(tokens, norm_gain, key_weight, key_cotangent, basis, exp_avg, exp_avg_sq)


def solution(mesh):
    in_specs = (
        P(("dp", "fsdp"), None),
        P(),
        P("fsdp", None),
        P(("dp", "fsdp"), None),
        P(),
        P("dp", "fsdp"),
        P("dp", "fsdp"),
    )
    out_specs = (P(("dp", "fsdp"), None), P("dp", "fsdp"), P("dp", "fsdp"), P("fsdp", None))
    return jax.shard_map(
        functools.partial(per_device, mesh.shape["dp"], mesh.shape["fsdp"]),
        mesh=mesh, in_specs=in_specs, out_specs=out_specs, check_vma=False,
    )
```
